512 devices in a mesh: dp: 16 (over z), row: 4 (over x), col: 8 (over y, core).
Axes of the slice: x: 4, y: 4, z: 16, core: 2. Of those that a mesh axis runs over, the one named last changes fastest.
Arguments:
- gradients: float32 [16, 2, 8192, 1024], P('dp', None, 'row', 'col'), may hold values from -20 to 20
- weight: float32 [2, 8192, 1024], P(None, 'row', 'col'), may hold values from -3 to 3
- row_state: float32 [2, 8192], P(None, 'row'), may hold values from 1e-06 to 30
- col_state: float32 [2, 1024], P(None, 'col'), may hold values from 1e-06 to 30
Outputs:
- new_weight: float32 [2, 8192, 1024], P(None, 'row', 'col')
- row_new: float32 [2, 8192], P(None, 'row')
- col_new: float32 [2, 1024], P(None, 'col')
The draws below stay inside these ranges and needn't reach their ends.
All inputs are finite; a program needn't handle non-finite values.
Results may differ from the reference program's by a relative error of at most 0.0003.
Values sent between devices are 32-bit elements; how exact they have to be, the bound alone decides.
No kernel may reach another device: no remote copies, remote signals or barrier semaphores. Data moves between devices by JAX's collectives and lax.ppermute only.
A program may use at most 64 MiB of HBM per device.

```python
import math
import jax
import jax.numpy as jnp
from jax import lax

D = 8192
KV = 1024
MATS = 2
REPLICAS = 16


def scales(key):
    row_key, col_key = jax.random.split(key)
    ramp_rows = jnp.arange(D, dtype=jnp.float32) / D
    ramp_cols = jnp.arange(KV, dtype=jnp.float32) / KV
    row_scale = jnp.exp(math.log(0.3) + math.log(10.0) * (0.7 * ramp_rows[None, :] + 0.3 * jax.random.uniform(row_key, (MATS, D))))
    col_scale = jnp.exp(math.log(0.3) + math.log(10.0) * (0.7 * ramp_cols[None, :] + 0.3 * jax.random.uniform(col_key, (MATS, KV))))
    return (row_scale, col_scale)


def matrix_scales():
    return jnp.where(jnp.arange(MATS) % 2 == 1, 0.15, 1.0).astype(jnp.float32)


def block_amplitude(key):
    table = jnp.exp(math.log(0.4) + math.log(3.25) * jax.random.uniform(key, (MATS, 16, 8)))
    table = jnp.repeat(table, D // 16, axis=1)
    return jnp.repeat(table, KV // 8, axis=2)


def draw_gradients(key, part):
    row_scale, col_scale = scales(key)
    key = jax.random.fold_in(key, 1)
    first_key = jax.random.fold_in(key, 0)
    amplitude = block_amplitude(jax.random.fold_in(key, 5))
    values = jnp.clip(jax.random.normal(first_key, (REPLICAS, MATS, D, KV)), -6.0, 6.0)
    matrix_scale = matrix_scales()
    return values * amplitude[None] * row_scale[None, :, :, None] * col_scale[None, :, None, :] * matrix_scale[None, :, None, None] * REPLICAS ** (-0.5)


def draw_row_state(key, part):
    row_scale, col_scale = scales(key)
    key = jax.random.fold_in(key, 2)
    ramp_rows = jnp.arange(D, dtype=jnp.float32) / D
    factor = jnp.exp(math.log(0.05) + math.log(30.0) * (0.8 * ramp_rows[None, :] + 0.2 * jax.random.uniform(key, (MATS, D))))
    matrix_scale = matrix_scales()
    return row_scale * row_scale * 0.5 * (matrix_scale * matrix_scale)[:, None] * factor


def draw_col_state(key, part):
    row_scale, col_scale = scales(key)
    key = jax.random.fold_in(key, 3)
    ramp_cols = jnp.arange(KV, dtype=jnp.float32) / KV
    factor = jnp.exp(math.log(0.05) + math.log(30.0) * (0.8 * ramp_cols[None, :] + 0.2 * jax.random.uniform(key, (MATS, KV))))
    matrix_scale = matrix_scales()
    multiplier = jnp.where(jnp.arange(MATS) % 2 == 1, 8.0, 0.2).astype(jnp.float32) * matrix_scale * matrix_scale
    return col_scale * col_scale * multiplier[:, None] * factor


def levels(rng, shape, cuts, least, largest):
    factor_of, own = 1.0, jax.random.fold_in(rng, 6)
    for position, parts in cuts:
        heights = jnp.exp(jax.random.uniform(jax.random.fold_in(own, position), (parts,), jnp.float32, least / len(cuts), largest / len(cuts)))
        factor_of = factor_of * jnp.repeat(heights, shape[position] // parts).reshape([-1 if axis == position else 1 for axis in range(len(shape))])
    return factor_of


def bell_draw(key, extent, scale, most, cuts=(), kind=jnp.bfloat16):
    drawn = scale * jax.random.normal(key, extent, jnp.float32)
    if cuts:
        drawn = drawn * levels(key, extent, cuts, -0.22, 0.18)
    return jnp.clip(drawn, -most, most).astype(kind)


def setup_inputs(seed: int = 0) -> dict:
    seeds = jax.random.split(jax.random.key(seed), 5)
    gradients = draw_gradients(jax.random.fold_in(seeds[4], 71), 0)
    weight = bell_draw(seeds[1], (MATS, D, KV), 0.5, 3.0, ((1, 4), (2, 8)), jnp.float32)
    row_state = draw_row_state(jax.random.fold_in(seeds[4], 71), 0)
    col_state = draw_col_state(jax.random.fold_in(seeds[4], 71), 0)
    return dict(gradients=gradients, weight=weight, row_state=row_state, col_state=col_state)


epsilon_one = 1e-30
decay_rate = 0.8
clip_limit = 1.0
step_size = 0.25

def reference(gradients, weight, row_state, col_state):
    summed = lax.optimization_barrier(jnp.sum(gradients, axis=0))
    squares = summed * summed + epsilon_one
    row_new = decay_rate * row_state + (1.0 - decay_rate) * lax.optimization_barrier(jnp.mean(squares, axis=2))
    col_new = decay_rate * col_state + (1.0 - decay_rate) * lax.optimization_barrier(jnp.mean(squares, axis=1))
    row_total = lax.optimization_barrier(jnp.sum(row_new, axis=1))
    second = row_new[:, :, None] * col_new[:, None, :] * (D / row_total)[:, None, None]
    update = summed * lax.rsqrt(second)
    mean_square = lax.optimization_barrier(jnp.mean(update * update, axis=(1, 2)))
    divisor = jnp.maximum(1.0, jnp.sqrt(mean_square) / clip_limit)
    new_weight = weight - step_size * update / divisor[:, None, None]
    return (new_weight, row_new, col_new)
```

```python
import jax
import jax.numpy as jnp
from jax import lax
from jax.sharding import PartitionSpec as P

D = 8192
KV = 1024

epsilon_one = 1e-30
decay_rate = 0.8
clip_limit = 1.0
step_size = 0.25


def statistics(part, row_state, col_state, rows):
    mats, count, width = part.shape
    squares = part * part + epsilon_one
    old = lax.dynamic_slice_in_dim(row_state, lax.axis_index("dp") * count, count, axis=1)
    row_part = jnp.sum(squares, axis=2)
    row_sum = jnp.sum(lax.all_gather(row_part, "col"), axis=0)
    row_fresh = decay_rate * old + (1.0 - decay_rate) * (row_sum / KV)
    col_part = jnp.sum(squares, axis=1)
    weighted = jnp.sum(squares * (1.0 / row_fresh)[:, :, None], axis=1)
    total = jnp.broadcast_to(jnp.sum(row_fresh, axis=1, keepdims=True), (mats, width))
    packed = jnp.concatenate([row_fresh, col_part, weighted, total], axis=0)
    everyone = lax.all_gather(packed, "dp")
    row_new = jnp.transpose(everyone[:, :mats], (1, 0, 2)).reshape(mats, rows)
    sums = jnp.sum(everyone[:, mats:], axis=0)
    sums = jnp.sum(lax.all_gather(sums, "row"), axis=0)
    col_sum, weighted, total = sums[:mats], sums[mats : 2 * mats], sums[2 * mats :]
    row_total = total[:, 0]
    col_new = decay_rate * col_state + (1.0 - decay_rate) * (col_sum / D)
    own = jnp.sum(weighted / col_new, axis=1)
    own = jnp.broadcast_to(own[:, None], (mats, width))
    ratio = jnp.sum(lax.all_gather(own, "col"), axis=0)[:, 0]
    mean_square = ratio * (row_total / D) / (D * KV)
    divisor = jnp.maximum(1.0, jnp.sqrt(mean_square) / clip_limit)
    scale = step_size * jnp.sqrt(row_total / D) / divisor
    return row_new, col_new, scale


def local(gradients, weight, row_state, col_state):
    mine = gradients[0]
    rows = mine.shape[1]
    part = lax.psum_scatter(mine, "dp", scatter_dimension=1, tiled=True)
    summed = lax.all_gather(part, "dp", axis=1, tiled=True)
    row_new, col_new, scale = statistics(part, row_state, col_state, rows)
    left = scale[:, None] * lax.rsqrt(row_new)
    right = lax.rsqrt(col_new)
    new_weight = weight - summed * left[:, :, None] * right[:, None, :]
    return (new_weight, row_new, col_new)


def solution(mesh):
    in_specs = (P("dp", None, "row", "col"), P(None, "row", "col"), P(None, "row"), P(None, "col"))
    out_specs = (P(None, "row", "col"), P(None, "row"), P(None, "col"))
    return jax.shard_map(local, mesh=mesh, in_specs=in_specs, out_specs=out_specs, check_vma=False)
```

```python
import jax
import jax.numpy as jnp
import numpy as np
from jax import lax
from jax.experimental import pallas as pl
from jax.experimental.pallas import tpu as pltpu
from jax.sharding import PartitionSpec as P

D = 8192
KV = 1024

epsilon_one = 1e-30
decay_rate = 0.8
clip_limit = 1.0
step_size = 0.25

REACH = (1, -1, 3, -5)


def partner(r, step, size, shift):
    r = (r - shift) % size
    r = r + REACH[step] if r % 2 == 0 else r - REACH[step]
    return (r + shift) % size


def owners(size, shift):
    def reach(r, step):
        if step == len(REACH):
            return frozenset([r])
        return reach(r, step + 1) | reach(partner(r, step, size, shift), step + 1)

    place, spans = [0] * size, [frozenset(range(size))]
    for step in range(len(REACH)):
        spans = [half for span in spans for half in (reach(min(span), step + 1), span - reach(min(span), step + 1))]
    for position, span in enumerate(spans):
        (only,) = span
        place[only] = position
    return place


def lookup(table, index):
    words = [sum(v << (4 * i) for i, v in enumerate(table[k : k + 7])) for k in (0, 7, 14)]
    word = jnp.where(index < 7, words[0], jnp.where(index < 14, words[1], words[2]))
    return (word >> (4 * (index % 7))) & 15


def halvings(x, place, shift, size):
    label = lookup(place, lax.axis_index("dp"))
    keep, base, count = x, jnp.int32(0), size
    arrived = None
    for step in range(len(REACH)):
        count //= 2
        bit = (label // count) % 2
        go, stay = (1 - bit) * count, bit * count
        take = lambda a, at: lax.dynamic_slice_in_dim(a, at, count, axis=0)
        if arrived is None:
            out = take(keep, go)
            base = stay
        else:
            out = take(keep, base + go) + take(arrived, go)
        pairs = [(r, partner(r, step, size, shift)) for r in range(size)]
        landed = lax.ppermute(out, "dp", pairs)
        if arrived is not None:
            keep, base = take(keep, base + stay) + take(arrived, stay), jnp.int32(0)
        arrived = landed
    return lax.dynamic_slice_in_dim(keep, base, 1, axis=0)[0] + arrived[0]


def statistics(part, row_state, col_state, places):
    mats, count, width = part.shape
    size = len(places[0])
    squares = part * part + epsilon_one
    me = lax.axis_index("dp")
    old = jnp.concatenate(
        [lax.dynamic_slice(row_state, (m, lookup(places[m], me) * count), (1, count)) for m in range(mats)], axis=0
    )
    row_part = jnp.sum(squares, axis=2)
    row_sum = jnp.sum(lax.all_gather(row_part, "col"), axis=0)
    row_fresh = decay_rate * old + (1.0 - decay_rate) * (row_sum / KV)
    col_part = jnp.sum(squares, axis=1)
    weighted = jnp.sum(squares * (1.0 / row_fresh)[:, :, None], axis=1)
    total = jnp.broadcast_to(jnp.sum(row_fresh, axis=1, keepdims=True), (mats, width))
    packed = jnp.concatenate([row_fresh, col_part, weighted, total], axis=0)
    everyone = lax.all_gather(packed, "dp")
    row_new = jnp.stack(
        [jnp.concatenate([everyone[place.index(b), m] for b in range(size)]) for m, place in enumerate(places)]
    )
    sums = jnp.sum(everyone[:, mats:], axis=0)
    sums = jnp.sum(lax.all_gather(sums, "row"), axis=0)
    col_sum, weighted, total = sums[:mats], sums[mats : 2 * mats], sums[2 * mats :]
    row_total = total[:, 0]
    col_new = decay_rate * col_state + (1.0 - decay_rate) * (col_sum / D)
    own = jnp.sum(weighted / col_new, axis=1)
    own = jnp.broadcast_to(own[:, None], (mats, width))
    ratio = jnp.sum(lax.all_gather(own, "col"), axis=0)[:, 0]
    mean_square = ratio * (row_total / D) / (D * KV)
    divisor = jnp.maximum(1.0, jnp.sqrt(mean_square) / clip_limit)
    scale = step_size * jnp.sqrt(row_total / D) / divisor
    return row_new, col_new, scale


GROUP = 4


def finish_kernel(table, left_ref, right_ref, *refs):
    blocks, weight_ref, out_ref = refs[:GROUP], refs[GROUP], refs[GROUP + 1]
    right = right_ref[0]
    columns = jnp.transpose(left_ref[0, 0])
    for k in range(GROUP):
        factor = columns[:, k : k + 1] * right[0:1]
        out_ref[0, k] = weight_ref[0, k] - blocks[k][0, 0] * factor


def finish(summed, weight, left, right, places):
    mats, size, rows, width = weight.shape
    table = jnp.asarray(np.array([[place.index(b) for b in range(size)] for place in places], np.int32))
    left = jnp.pad(left.reshape(mats, size // GROUP, GROUP, rows), ((0, 0), (0, 0), (0, 8 - GROUP), (0, 0)))
    right = jnp.broadcast_to(right[:, None, :], (mats, 8, width))
    block = lambda k: pl.BlockSpec((1, 1, rows, width), lambda m, g, t: (m, t[m, g * GROUP + k], 0, 0))
    tile = pl.BlockSpec((1, GROUP, rows, width), lambda m, g, t: (m, g, 0, 0))
    return pl.pallas_call(
        finish_kernel,
        grid_spec=pltpu.PrefetchScalarGridSpec(
            num_scalar_prefetch=1,
            grid=(mats, size // GROUP),
            in_specs=[
                pl.BlockSpec((1, 1, 8, rows), lambda m, g, t: (m, g, 0, 0)),
                pl.BlockSpec((1, 8, width), lambda m, g, t: (m, 0, 0)),
            ]
            + [block(k) for k in range(GROUP)]
            + [tile],
            out_specs=tile,
        ),
        out_shape=jax.ShapeDtypeStruct(weight.shape, weight.dtype),
    )(table, left, right, *[summed] * GROUP, weight)


def local(gradients, weight, row_state, col_state):
    mats, rows, width = weight.shape
    size = lax.axis_size("dp")
    places = [owners(size, m) for m in range(mats)]
    mine = gradients.reshape(mats, size, rows // size, width)
    part = jnp.stack([halvings(mine[m], places[m], m, size) for m in range(mats)])
    summed = lax.all_gather(part, "dp", axis=1, tiled=True)
    row_new, col_new, scale = statistics(part, row_state, col_state, places)
    left = scale[:, None] * lax.rsqrt(row_new)
    right = lax.rsqrt(col_new)
    blocks = lambda a: a.reshape(mats, size, rows // size, width)
    new_weight = finish(blocks(summed), blocks(weight), left, right, places).reshape(weight.shape)
    return (new_weight, row_new, col_new)


def solution(mesh):
    in_specs = (P("dp", None, "row", "col"), P(None, "row", "col"), P(None, "row"), P(None, "col"))
    out_specs = (P(None, "row", "col"), P(None, "row"), P(None, "col"))
    return jax.shard_map(local, mesh=mesh, in_specs=in_specs, out_specs=out_specs, check_vma=False)
```

```python
import functools

import jax
import jax.numpy as jnp
from jax import lax
from jax.experimental import pallas as pl
from jax.experimental.layout import Layout, with_layout_constraint
from jax.experimental.pallas import tpu as pltpu
from jax.sharding import PartitionSpec as P

D = 8192
KV = 1024

epsilon_one = 1e-30
decay_rate = 0.8
clip_limit = 1.0
step_size = 0.25

REACH = (1, -1, 3, -5)


def partner(r, step, size, core):
    r = (r - core) % size
    r = r + REACH[step] if r % 2 == 0 else r - REACH[step]
    return (r + core) % size


def owners(size):
    def reach(r, step):
        if step == len(REACH):
            return frozenset([r])
        return reach(r, step + 1) | reach(partner(r, step, size, 0), step + 1)

    place, spans = [0] * size, [frozenset(range(size))]
    for step in range(len(REACH)):
        spans = [half for span in spans for half in (reach(min(span), step + 1), span - reach(min(span), step + 1))]
    for position, span in enumerate(spans):
        (only,) = span
        place[only] = position
    return place


def lookup(table, index):
    words = [sum(v << (4 * i) for i, v in enumerate(table[k : k + 7])) for k in (0, 7, 14)]
    word = jnp.where(index < 7, words[0], jnp.where(index < 14, words[1], words[2]))
    part = jnp.where(index < 7, index, jnp.where(index < 14, index - 7, index - 14))
    return (word >> (4 * part)) & 15


def plain(x):
    return with_layout_constraint(x, Layout(major_to_minor=tuple(range(x.ndim))))


def exchange(x, target, size, cols):
    pairs = []
    for r in range(size):
        for c in range(cols):
            other, core = target(r, c % 2)
            pairs.append((r * cols + c, other * cols + c - c % 2 + core))
    return lax.ppermute(x, ("dp", "col"), pairs)


def halvings(x, label, size, cols):
    keep, base, count, arrived = x, jnp.int32(0), size, None
    for step in range(len(REACH)):
        count //= 2
        bit = (label // count) & 1
        go, stay = (1 - bit) * count, bit * count
        take = lambda a, at: lax.dynamic_slice_in_dim(a, at, count, axis=1)
        if arrived is None:
            out = take(keep, go)
            base = stay
        else:
            out = take(keep, base + go) + take(arrived, go)
        out = plain(out[:, 0] if count == 1 else out)
        landed = exchange(out, lambda r, core: (partner(r, step, size, core), core), size, cols)
        if arrived is not None:
            keep, base = take(keep, base + stay) + take(arrived, stay), jnp.int32(0)
        arrived = plain(landed)
    return lax.optimization_barrier(lax.dynamic_slice_in_dim(keep, base, 1, axis=1)[:, 0] + arrived)


def statistics(part, row_state, col_state, label, core, place, cols):
    mats, count, width = part.shape
    size = len(place)
    squares = part * part + epsilon_one
    old = lax.dynamic_slice(row_state, (0, label * count), (mats, count))
    row_part = lax.all_gather(jnp.sum(squares, axis=2), "col")
    row_part = row_part.reshape(cols // 2, 2, mats, count)
    own = jnp.sum(jnp.where(core == 0, row_part[:, 0], row_part[:, 1]), axis=0)
    other = exchange(own, lambda r, c: ((r + 1 - 2 * c) % size, 1 - c), size, cols)
    row_fresh = decay_rate * old + (1.0 - decay_rate) * ((own + other) / KV)
    col_part = jnp.sum(squares, axis=1)
    weighted = jnp.sum(squares * (1.0 / row_fresh)[:, :, None], axis=1)
    total = jnp.broadcast_to(jnp.sum(row_fresh, axis=1, keepdims=True), (mats, width))
    packed = jnp.concatenate([row_fresh, col_part, weighted, total], axis=0)
    everyone = lax.all_gather(packed, "dp")
    fresh = everyone[:, :mats]
    fresh = jnp.where(core == 0, fresh, jnp.roll(fresh, -1, axis=0))
    row_new = jnp.stack([fresh[place.index(b)] for b in range(size)], axis=1)
    sums = jnp.sum(everyone[:, mats:], axis=0)
    sums = jnp.sum(lax.all_gather(sums, "row"), axis=0)
    col_sum, weighted, total = sums[:mats], sums[mats : 2 * mats], sums[2 * mats :]
    row_total = total[:, 0]
    col_new = decay_rate * col_state + (1.0 - decay_rate) * (col_sum / D)
    share = jnp.sum(weighted / col_new, axis=1)
    share = jnp.broadcast_to(share[:, None], (mats, width))
    ratio = jnp.sum(lax.all_gather(share, "col"), axis=0)[:, 0]
    mean_square = ratio * (row_total / D) / (D * KV)
    divisor = jnp.maximum(1.0, jnp.sqrt(mean_square) / clip_limit)
    scale = step_size * jnp.sqrt(row_total / D) / divisor
    return row_new, col_new, scale


def finish_kernel(place, core_ref, left_ref, right_ref, weight_ref, summed_ref, out_ref, held, in_sem, out_sem):
    size = len(place)

    def arrival(b):
        source = (place.index(b) + core_ref[0]) & (size - 1)
        return pltpu.make_async_copy(summed_ref.at[source], held.at[:, b], in_sem.at[b])

    def departure(b):
        return pltpu.make_async_copy(held.at[:, b], out_ref.at[:, b], out_sem.at[b])

    for b in range(size):
        arrival(b).start()
    mats = weight_ref.shape[0]
    columns = [jnp.transpose(left_ref[m]) for m in range(mats)]
    for b in range(size):
        arrival(b).wait()
        for m in range(mats):
            factor = columns[m][:, b : b + 1] * right_ref[m : m + 1]
            held[m, b] = weight_ref[m, b] - held[m, b] * factor
        departure(b).start()
    for b in range(size):
        departure(b).wait()


def finish(summed, weight, left, right, core, place):
    whole = lambda space: pl.BlockSpec(memory_space=space)
    return pl.pallas_call(
        functools.partial(finish_kernel, place),
        in_specs=[whole(pltpu.SMEM)] + [whole(pltpu.VMEM)] * 3 + [whole(pltpu.HBM)],
        out_specs=whole(pltpu.HBM),
        out_shape=jax.ShapeDtypeStruct(weight.shape, weight.dtype),
        scratch_shapes=[
            pltpu.VMEM(weight.shape, weight.dtype),
            pltpu.SemaphoreType.DMA((len(place),)),
            pltpu.SemaphoreType.DMA((len(place),)),
        ],
        compiler_params=pltpu.CompilerParams(vmem_limit_bytes=60 << 20),
        cost_estimate=pl.CostEstimate(flops=2**21, bytes_accessed=6 * 2**20, transcendentals=0),
    )(core.reshape(1), left, right, weight, summed)


def local(gradients, weight, row_state, col_state):
    mats, rows, width = weight.shape
    size, cols = lax.axis_size("dp"), lax.axis_size("col")
    place = owners(size)
    core = lax.axis_index("col") & 1
    label = lookup(place, (lax.axis_index("dp") - core) & (size - 1))
    blocks = lambda a: a.reshape(mats, size, rows // size, width)
    part = halvings(blocks(gradients), label, size, cols)
    summed = lax.all_gather(part, "dp")
    row_new, col_new, scale = statistics(part, row_state, col_state, label, core, place, cols)
    left = scale[:, None, None] * lax.rsqrt(row_new)
    right = lax.rsqrt(col_new)
    new_weight = finish(summed, blocks(weight), left, right, core, place).reshape(weight.shape)
    return (new_weight, row_new.reshape(mats, rows), col_new)


def solution(mesh):
    in_specs = (P("dp", None, "row", "col"), P(None, "row", "col"), P(None, "row"), P(None, "col"))
    out_specs = (P(None, "row", "col"), P(None, "row"), P(None, "col"))
    return jax.shard_map(local, mesh=mesh, in_specs=in_specs, out_specs=out_specs, check_vma=False)
```

```python
import functools

import jax
import jax.numpy as jnp
from jax import lax
from jax.experimental import pallas as pl
from jax.experimental.layout import Layout, with_layout_constraint
from jax.experimental.pallas import tpu as pltpu
from jax.sharding import PartitionSpec as P

D = 8192
KV = 1024

epsilon_one = 1e-30
decay_rate = 0.8
clip_limit = 1.0
step_size = 0.25

CLASSES = 4
HOPS = (2, 1, -1)
STEPS = (3, -5)
BACK = tuple(hop if hop % 2 else -hop for hop in HOPS)


def target(r, hop, size):
    return (r + hop if r % 2 == 0 else r - hop) % size


def owners(size):
    place, free = {}, 0
    for r in range(0, size, 2):
        if r not in place:
            other = target(r, STEPS[0], size)
            for q in (r, target(r, STEPS[1], size), other, target(other, STEPS[1], size)):
                place[q], free = free, free + 1
    return [place[r] for r in range(size)]


def lookup(table, index):
    words = [sum(v << (4 * i) for i, v in enumerate(table[k : k + 7])) for k in (0, 7, 14)]
    word = jnp.where(index < 7, words[0], jnp.where(index < 14, words[1], words[2]))
    part = jnp.where(index < 7, index, jnp.where(index < 14, index - 7, index - 14))
    return (word >> (4 * part)) & 15


def plain(x):
    return with_layout_constraint(x, Layout(major_to_minor=tuple(range(x.ndim))))


def reach(x, hop, size):
    return plain(lax.ppermute(plain(x), "dp", [(r, target(r, hop, size)) for r in range(size)]))


def spread(x, place, me):
    size = len(place)
    quarter = size // CLASSES
    mine = lookup(place, me)
    take = lambda which: lax.dynamic_slice_in_dim(x, which * quarter, quarter, axis=1)
    landed = [
        reach(take(lookup([place[target(r, hop, size)] // quarter for r in range(size)], me)), hop, size) for hop in HOPS
    ]
    held = plain(lax.optimization_barrier(take(mine // quarter) + landed[0] + landed[1] + landed[2]))
    half, last = (mine // 2) & 1, mine & 1
    two = lambda a, at: lax.dynamic_slice_in_dim(a, at, 2, axis=1)
    one = lambda a, at: lax.dynamic_index_in_dim(a, at, axis=1, keepdims=False)
    landed = reach(two(held, 2 - 2 * half), STEPS[0], size)
    out = one(held, 2 * half + 1 - last) + one(landed, 1 - last)
    keep = one(held, 2 * half + last) + one(landed, last)
    return lax.optimization_barrier(keep + reach(out, STEPS[1], size))


def join(own, other, bit):
    return jnp.where(bit == 0, jnp.concatenate([own, other]), jnp.concatenate([other, own]))


def pairs_of(part, place, me):
    return plain(join(part[None], reach(part, STEPS[1], len(place))[None], lookup(place, me) & 1))


def class_of(pair, place, me):
    return plain(join(pair, reach(pair, STEPS[0], len(place)), (lookup(place, me) // 2) & 1))


def after(x, other):
    return x + 0.0 * other[0, 0, : x.shape[0]]


def row_statistics(part, row_state, mine):
    mats, count, width = part.shape
    squares = part * part + epsilon_one
    old = lax.dynamic_slice(row_state, (0, mine * count), (mats, count))
    row_sum = jnp.sum(lax.all_gather(jnp.sum(squares, axis=2), "col"), axis=0)
    row_fresh = decay_rate * old + (1.0 - decay_rate) * (row_sum / KV)
    col_part = jnp.sum(squares, axis=1)
    weighted = jnp.sum(squares * (1.0 / row_fresh)[:, :, None], axis=1)
    total = jnp.broadcast_to(jnp.sum(row_fresh, axis=1, keepdims=True), (mats, width))
    return jnp.concatenate([row_fresh, col_part, weighted, total], axis=0)


def col_statistics(sums, col_state):
    mats, width = col_state.shape
    sums = jnp.sum(lax.all_gather(sums, "row"), axis=0)
    row_total = sums[2 * mats :, 0]
    col_new = decay_rate * col_state + (1.0 - decay_rate) * (sums[:mats] / D)
    shares = lax.all_gather(sums[mats : 2 * mats] / col_new, "col")
    ratio = jnp.sum(shares, axis=(0, 2))
    mean_square = ratio * (row_total / D) / (D * KV)
    divisor = jnp.maximum(1.0, jnp.sqrt(mean_square) / clip_limit)
    scale = step_size * jnp.sqrt(row_total / D) / divisor
    return col_new, scale


def finish_kernel(place, class_ref, scale_ref, every_ref, right_ref, weight_ref, *refs):
    parts, (out_ref, row_ref, held, left_ref, sems) = refs[:CLASSES], refs[CLASSES:]
    mats, _, blocks, rows, _ = weight_ref.shape
    for b in range(CLASSES * blocks):
        fresh = every_ref[place.index(b), 0:mats]
        row_ref[:, b] = fresh
        left_ref[b // blocks, b % blocks * mats : (b % blocks + 1) * mats] = lax.rsqrt(fresh)
    right = [right_ref[m : m + 1] * scale_ref[m] for m in range(mats)]
    copies = []
    for k in range(CLASSES):
        which = class_ref[k]
        columns = jnp.transpose(left_ref[which])
        for b in range(blocks):
            for m in range(mats):
                factor = columns[:, b * mats + m : b * mats + m + 1] * right[m]
                held[k, m, b] = weight_ref[m, which, b] - parts[k][b, m] * factor
        copies.append(pltpu.make_async_copy(held.at[k], out_ref.at[:, which], sems.at[k]))
        copies[-1].start()
    for copy in copies:
        copy.wait()


def finish(place, parts, weight, everyone, right, scale, classes):
    whole = lambda space: pl.BlockSpec(memory_space=space)
    mats, _, blocks, rows, width = weight.shape
    return pl.pallas_call(
        functools.partial(finish_kernel, place),
        in_specs=[whole(pltpu.SMEM)] * 2 + [whole(pltpu.VMEM)] * (3 + CLASSES),
        out_specs=[whole(pltpu.HBM), whole(pltpu.VMEM)],
        out_shape=[
            jax.ShapeDtypeStruct(weight.shape, weight.dtype),
            jax.ShapeDtypeStruct((mats, CLASSES * blocks, rows), weight.dtype),
        ],
        scratch_shapes=[
            pltpu.VMEM((CLASSES, mats, blocks, rows, width), weight.dtype),
            pltpu.VMEM((CLASSES, blocks * mats, rows), weight.dtype),
            pltpu.SemaphoreType.DMA((CLASSES,)),
        ],
        compiler_params=pltpu.CompilerParams(vmem_limit_bytes=20 << 20),
        cost_estimate=pl.CostEstimate(flops=2**21, bytes_accessed=6 * 2**20, transcendentals=0),
    )(classes, scale, everyone, right, weight, *parts)


def local(gradients, weight, row_state, col_state):
    mats, rows, width = weight.shape
    size, me = lax.axis_size("dp"), lax.axis_index("dp")
    blocks, count = size // CLASSES, rows // size
    place = owners(size)
    part = spread(gradients.reshape(mats, size, count, width), place, me)
    extra = row_statistics(part, row_state, lookup(place, me))
    pair = pairs_of(part, place, me)
    everyone = lax.all_gather(after(extra, pair), "dp")
    own = class_of(pair, place, me)
    parts = [own] + [reach(own, hop, size) for hop in BACK]
    col_new, scale = col_statistics(after(jnp.sum(everyone, axis=0)[mats:], own), col_state)
    classes = [lookup([p // blocks for p in place], me)]
    for hop in BACK:
        source = {target(r, hop, size): r for r in range(size)}
        classes.append(lookup([place[source[r]] // blocks for r in range(size)], me))
    split = weight.reshape(mats, CLASSES, blocks, count, width)
    new_weight, row_new = finish(place, parts, split, everyone, lax.rsqrt(col_new), scale, jnp.stack(classes))
    return (new_weight.reshape(weight.shape), row_new.reshape(mats, rows), col_new)


def solution(mesh):
    in_specs = (P("dp", None, "row", "col"), P(None, "row", "col"), P(None, "row"), P(None, "col"))
    out_specs = (P(None, "row", "col"), P(None, "row"), P(None, "col"))
    return jax.shard_map(local, mesh=mesh, in_specs=in_specs, out_specs=out_specs, check_vma=False)
```

```python
import functools

import jax
import jax.numpy as jnp
from jax import lax
from jax.experimental import pallas as pl
from jax.experimental.layout import Layout, with_layout_constraint
from jax.experimental.pallas import tpu as pltpu
from jax.sharding import PartitionSpec as P

D = 8192
KV = 1024

epsilon_one = 1e-30
decay_rate = 0.8
clip_limit = 1.0
step_size = 0.25

CLASSES = 4
HOPS = (2, 1, -1)
STEPS = (3, -5)
BACK = tuple(hop if hop % 2 else -hop for hop in HOPS)


def target(r, hop, size):
    return (r + hop if r % 2 == 0 else r - hop) % size


def owners(size):
    place, free = {}, 0
    for r in range(0, size, 2):
        if r not in place:
            other = target(r, STEPS[0], size)
            for q in (r, target(r, STEPS[1], size), other, target(other, STEPS[1], size)):
                place[q], free = free, free + 1
    return [place[r] for r in range(size)]


def lookup(table, index):
    words = [sum(v << (4 * i) for i, v in enumerate(table[k : k + 7])) for k in (0, 7, 14)]
    word = jnp.where(index < 7, words[0], jnp.where(index < 14, words[1], words[2]))
    part = jnp.where(index < 7, index, jnp.where(index < 14, index - 7, index - 14))
    return (word >> (4 * part)) & 15


def plain(x):
    return with_layout_constraint(x, Layout(major_to_minor=tuple(range(x.ndim))))


def reach(x, hop, size):
    return plain(lax.ppermute(plain(x), "dp", [(r, target(r, hop, size)) for r in range(size)]))


def spread(x, place, me):
    size = len(place)
    quarter = size // CLASSES
    mine = lookup(place, me)
    take = lambda which: lax.dynamic_slice_in_dim(x, which * quarter, quarter, axis=1)
    landed = [
        reach(take(lookup([place[target(r, hop, size)] // quarter for r in range(size)], me)), hop, size) for hop in HOPS
    ]
    held = plain(lax.optimization_barrier(take(mine // quarter) + landed[0] + landed[1] + landed[2]))
    half, last = (mine // 2) & 1, mine & 1
    two = lambda a, at: lax.dynamic_slice_in_dim(a, at, 2, axis=1)
    one = lambda a, at: lax.dynamic_index_in_dim(a, at, axis=1, keepdims=False)
    landed = reach(two(held, 2 - 2 * half), STEPS[0], size)
    out = one(held, 2 * half + 1 - last) + one(landed, 1 - last)
    keep = one(held, 2 * half + last) + one(landed, last)
    return lax.optimization_barrier(keep + reach(out, STEPS[1], size))


def join(own, other, bit):
    return jnp.where(bit == 0, jnp.concatenate([own, other]), jnp.concatenate([other, own]))


def pairs_of(part, place, me):
    return plain(join(part[None], reach(part, STEPS[1], len(place))[None], lookup(place, me) & 1))


def class_of(pair, place, me):
    return plain(join(pair, reach(pair, STEPS[0], len(place)), (lookup(place, me) // 2) & 1))


def class_statistics(own, row_state, which):
    blocks, mats, count, width = own.shape
    squares = own * own + epsilon_one
    old = lax.dynamic_index_in_dim(row_state.reshape(mats, CLASSES, blocks, count), which, axis=1, keepdims=False)
    row_sum = jnp.sum(lax.all_gather(jnp.sum(squares, axis=3), "col"), axis=0)
    row_fresh = decay_rate * jnp.transpose(old, (1, 0, 2)) + (1.0 - decay_rate) * (row_sum / KV)
    col_part = jnp.sum(squares, axis=(0, 2))
    weighted = jnp.sum(squares * (1.0 / row_fresh)[..., None], axis=(0, 2))
    total = jnp.broadcast_to(jnp.sum(row_fresh, axis=(0, 2))[:, None], (mats, width))
    return jnp.concatenate([row_fresh.reshape(blocks * mats, width), col_part, weighted, total, jnp.zeros_like(total)])


def col_statistics(sums, col_state):
    mats, width = col_state.shape
    sums = jnp.sum(lax.all_gather(sums, "row"), axis=0)
    row_total = sums[2 * mats :, 0]
    col_new = decay_rate * col_state + (1.0 - decay_rate) * (sums[:mats] / D)
    shares = lax.all_gather(sums[mats : 2 * mats] / col_new, "col")
    ratio = jnp.sum(shares, axis=(0, 2))
    mean_square = ratio * (row_total / D) / (D * KV)
    divisor = jnp.maximum(1.0, jnp.sqrt(mean_square) / clip_limit)
    scale = step_size * jnp.sqrt(row_total / D) / divisor
    return col_new, scale


def finish_kernel(class_ref, scale_ref, small_ref, right_ref, weight_ref, *refs):
    parts, (out_ref, held, sems) = refs[:CLASSES], refs[CLASSES:]
    mats, _, blocks, rows, _ = weight_ref.shape
    right = [right_ref[m : m + 1] * scale_ref[m] for m in range(mats)]
    copies = []
    for k in range(CLASSES):
        which = class_ref[k]
        columns = jnp.transpose(lax.rsqrt(small_ref[k, 0 : blocks * mats]))
        for b in range(blocks):
            for m in range(mats):
                factor = columns[:, b * mats + m : b * mats + m + 1] * right[m]
                held[k, m, b] = weight_ref[m, which, b] - parts[k][b, m] * factor
        copies.append(pltpu.make_async_copy(held.at[k], out_ref.at[:, which], sems.at[k]))
        copies[-1].start()
    for copy in copies:
        copy.wait()


def finish(parts, weight, smalls, right, scale, classes):
    whole = lambda space: pl.BlockSpec(memory_space=space)
    mats, _, blocks, rows, width = weight.shape
    return pl.pallas_call(
        finish_kernel,
        in_specs=[whole(pltpu.SMEM)] * 2 + [whole(pltpu.VMEM)] * (3 + CLASSES),
        out_specs=whole(pltpu.HBM),
        out_shape=jax.ShapeDtypeStruct(weight.shape, weight.dtype),
        scratch_shapes=[
            pltpu.VMEM((CLASSES, mats, blocks, rows, width), weight.dtype),
            pltpu.SemaphoreType.DMA((CLASSES,)),
        ],
        compiler_params=pltpu.CompilerParams(vmem_limit_bytes=20 << 20),
        cost_estimate=pl.CostEstimate(flops=2**21, bytes_accessed=6 * 2**20, transcendentals=0),
    )(classes, scale, smalls, right, weight, *parts)


def local(gradients, weight, row_state, col_state):
    mats, rows, width = weight.shape
    size, me = lax.axis_size("dp"), lax.axis_index("dp")
    blocks, count = size // CLASSES, rows // size
    place = owners(size)
    part = spread(gradients.reshape(mats, size, count, width), place, me)
    own = class_of(pairs_of(part, place, me), place, me)
    parts = [own] + [reach(own, hop, size) for hop in BACK]
    classes = [lookup([p // blocks for p in place], me)]
    for hop in BACK:
        source = {target(r, hop, size): r for r in range(size)}
        classes.append(lookup([place[source[r]] // blocks for r in range(size)], me))
    small = class_statistics(own, row_state, classes[0])
    smalls = jnp.stack([small] + [reach(small, hop, size) for hop in BACK])
    placed = jnp.stack(classes)[None, :] == jnp.arange(CLASSES)[:, None]
    smalls_placed = jnp.sum(jnp.where(placed[:, :, None, None], smalls[None], 0.0), axis=1)
    fresh = smalls_placed[:, : blocks * mats].reshape(size, mats, count)
    sums = jnp.sum(smalls_placed[:, blocks * mats : (blocks + 3) * mats], axis=0)
    col_new, scale = col_statistics(sums, col_state)
    split = weight.reshape(mats, CLASSES, blocks, count, width)
    new_weight = finish(parts, split, smalls, lax.rsqrt(col_new), scale, jnp.stack(classes))
    row_new = jnp.transpose(fresh, (1, 0, 2)).reshape(mats, rows)
    return (new_weight.reshape(weight.shape), row_new, col_new)


def solution(mesh):
    in_specs = (P("dp", None, "row", "col"), P(None, "row", "col"), P(None, "row"), P(None, "col"))
    out_specs = (P(None, "row", "col"), P(None, "row"), P(None, "col"))
    return jax.shard_map(local, mesh=mesh, in_specs=in_specs, out_specs=out_specs, check_vma=False)
```

```python
import functools

import jax
import jax.numpy as jnp
from jax import lax
from jax.experimental import pallas as pl
from jax.experimental.layout import Layout, with_layout_constraint
from jax.experimental.pallas import tpu as pltpu
from jax.sharding import PartitionSpec as P

D = 8192
KV = 1024

epsilon_one = 1e-30
decay_rate = 0.8
clip_limit = 1.0
step_size = 0.25

CLASSES = 4
HOPS = (2, 1, -1)
STEPS = (3, -5)
BACK = tuple(hop if hop % 2 else -hop for hop in HOPS)


def target(r, hop, size):
    return (r + hop if r % 2 == 0 else r - hop) % size


def owners(size):
    place, free = {}, 0
    for r in range(0, size, 2):
        if r not in place:
            other = target(r, STEPS[0], size)
            for q in (target(r, STEPS[1], size), r, other, target(other, STEPS[1], size)):
                place[q], free = free, free + 1
    return [place[r] for r in range(size)]


def lookup(table, index):
    words = [sum(v << (4 * i) for i, v in enumerate(table[k : k + 7])) for k in (0, 7, 14)]
    word = jnp.where(index < 7, words[0], jnp.where(index < 14, words[1], words[2]))
    part = jnp.where(index < 7, index, jnp.where(index < 14, index - 7, index - 14))
    return (word >> (4 * part)) & 15


def plain(x):
    return with_layout_constraint(x, Layout(major_to_minor=tuple(range(x.ndim))))


def reach(x, hop, size):
    return plain(lax.ppermute(plain(x), "dp", [(r, target(r, hop, size)) for r in range(size)]))


def spread(x, place, me):
    size = len(place)
    quarter = size // CLASSES
    mine = lookup(place, me)
    take = lambda which: lax.dynamic_slice_in_dim(x, which * quarter, quarter, axis=1)
    landed = [
        reach(take(lookup([place[target(r, hop, size)] // quarter for r in range(size)], me)), hop, size) for hop in HOPS
    ]
    held = plain(lax.optimization_barrier(take(mine // quarter) + landed[0] + landed[1] + landed[2]))
    half, last = (mine // 2) & 1, mine & 1
    two = lambda a, at: lax.dynamic_slice_in_dim(a, at, 2, axis=1)
    one = lambda a, at: lax.dynamic_index_in_dim(a, at, axis=1, keepdims=False)
    landed = reach(two(held, 2 - 2 * half), STEPS[0], size)
    out = one(held, 2 * half + 1 - last) + one(landed, 1 - last)
    keep = one(held, 2 * half + last) + one(landed, last)
    return lax.optimization_barrier(keep + reach(out, STEPS[1], size))


def row_statistics(part, row_state, mine):
    mats, count, width = part.shape
    squares = part * part + epsilon_one
    old = lax.dynamic_slice(row_state, (0, mine * count), (mats, count))
    row_sum = jnp.sum(lax.all_gather(jnp.sum(squares, axis=2), "col"), axis=0)
    row_fresh = decay_rate * old + (1.0 - decay_rate) * (row_sum / KV)
    col_part = jnp.sum(squares, axis=1)
    weighted = jnp.sum(squares * (1.0 / row_fresh)[:, :, None], axis=1)
    total = jnp.broadcast_to(jnp.sum(row_fresh, axis=1, keepdims=True), (mats, width))
    return jnp.concatenate([row_fresh, col_part, weighted, total], axis=0)


def col_statistics(sums, col_state):
    mats, width = col_state.shape
    sums = jnp.sum(lax.all_gather(sums, "row"), axis=0)
    row_total = sums[2 * mats :, 0]
    col_new = decay_rate * col_state + (1.0 - decay_rate) * (sums[:mats] / D)
    shares = lax.all_gather(sums[mats : 2 * mats] / col_new, "col")
    ratio = jnp.sum(shares, axis=(0, 2))
    mean_square = ratio * (row_total / D) / (D * KV)
    divisor = jnp.maximum(1.0, jnp.sqrt(mean_square) / clip_limit)
    scale = step_size * jnp.sqrt(row_total / D) / divisor
    return col_new, scale


def finish_kernel(class_ref, scale_ref, left_ref, right_ref, weight_ref, *refs):
    parts, out_ref, held, sems = refs[:CLASSES], refs[CLASSES], refs[CLASSES + 1], refs[CLASSES + 2]
    mats, _, blocks, rows, _ = weight_ref.shape
    right = [right_ref[m : m + 1] * scale_ref[m] for m in range(mats)]
    copies = []
    for k in range(CLASSES):
        which = class_ref[k]
        columns = jnp.transpose(left_ref[k])
        for b in range(blocks):
            for m in range(mats):
                factor = columns[:, b * mats + m : b * mats + m + 1] * right[m]
                held[k, m, b] = weight_ref[m, which, b] - parts[k][b, m * rows : (m + 1) * rows] * factor
        copies.append(pltpu.make_async_copy(held.at[k], out_ref.at[:, which], sems.at[k]))
        copies[-1].start()
    for copy in copies:
        copy.wait()


def finish(parts, weight, left, right, scale, classes):
    whole = lambda space: pl.BlockSpec(memory_space=space)
    mats, _, blocks, rows, width = weight.shape
    return pl.pallas_call(
        finish_kernel,
        in_specs=[whole(pltpu.SMEM)] * 2 + [whole(pltpu.VMEM)] * (3 + CLASSES),
        out_specs=whole(pltpu.HBM),
        out_shape=jax.ShapeDtypeStruct(weight.shape, weight.dtype),
        scratch_shapes=[
            pltpu.VMEM((CLASSES, mats, blocks, rows, width), weight.dtype),
            pltpu.SemaphoreType.DMA((CLASSES,)),
        ],
        compiler_params=pltpu.CompilerParams(vmem_limit_bytes=20 << 20),
        cost_estimate=pl.CostEstimate(flops=2**21, bytes_accessed=6 * 2**20, transcendentals=0),
    )(classes, scale, left, right, weight, *parts)


def local(gradients, weight, row_state, col_state):
    mats, rows, width = weight.shape
    size, me = lax.axis_size("dp"), lax.axis_index("dp")
    blocks, count = size // CLASSES, rows // size
    place = owners(size)
    part = spread(gradients.reshape(mats, size, count, width), place, me)
    extra = row_statistics(part, row_state, lookup(place, me))
    sent = jnp.concatenate([part.reshape(mats * count, width), extra], axis=0)
    members = [[place.index(c * blocks + b) for b in range(blocks)] for c in range(CLASSES)]
    own = lax.all_gather(sent, "dp", axis_index_groups=members)
    small = lax.optimization_barrier(own[:, mats * count :])
    smalls = jnp.stack([small] + [reach(small, hop, size) for hop in BACK])
    parts = [own] + [reach(own, hop, size) for hop in BACK]
    classes = [lookup([p // blocks for p in place], me)]
    for hop in BACK:
        source = {target(r, hop, size): r for r in range(size)}
        classes.append(lookup([place[source[r]] // blocks for r in range(size)], me))
    placed = jnp.stack(classes)[None, :] == jnp.arange(CLASSES)[:, None]
    smalls_placed = jnp.sum(jnp.where(placed[:, :, None, None, None], smalls[None], 0.0), axis=1)
    row_new = jnp.transpose(smalls_placed[:, :, :mats].reshape(size, mats, count), (1, 0, 2)).reshape(mats, rows)
    col_new, scale = col_statistics(jnp.sum(smalls_placed[:, :, mats:], axis=(0, 1)), col_state)
    left = lax.rsqrt(smalls[:, :, :mats]).reshape(CLASSES, blocks * mats, count)
    split = weight.reshape(mats, CLASSES, blocks, count, width)
    new_weight = finish(parts, split, left, lax.rsqrt(col_new), scale, jnp.stack(classes))
    return (new_weight.reshape(weight.shape), row_new, col_new)


def solution(mesh):
    in_specs = (P("dp", None, "row", "col"), P(None, "row", "col"), P(None, "row"), P(None, "col"))
    out_specs = (P(None, "row", "col"), P(None, "row"), P(None, "col"))
    return jax.shard_map(local, mesh=mesh, in_specs=in_specs, out_specs=out_specs, check_vma=False)
```

```python
import functools

import jax
import jax.numpy as jnp
from jax import lax
from jax.experimental import pallas as pl
from jax.experimental.layout import Layout, with_layout_constraint
from jax.experimental.pallas import tpu as pltpu
from jax.sharding import PartitionSpec as P

D = 8192
KV = 1024

epsilon_one = 1e-30
decay_rate = 0.8
clip_limit = 1.0
step_size = 0.25

CLASSES = 4
HOPS = (2, 1, -1)
STEPS = (3, -5)
BACK = tuple(hop if hop % 2 else -hop for hop in HOPS)


def target(r, hop, size):
    return (r + hop if r % 2 == 0 else r - hop) % size


def owners(size):
    place, free = {}, 0
    for r in range(0, size, 2):
        if r not in place:
            other = target(r, STEPS[0], size)
            for q in (target(r, STEPS[1], size), r, other, target(other, STEPS[1], size)):
                place[q], free = free, free + 1
    return [place[r] for r in range(size)]


def lookup(table, index):
    words = [sum(v << (4 * i) for i, v in enumerate(table[k : k + 7])) for k in (0, 7, 14)]
    word = jnp.where(index < 7, words[0], jnp.where(index < 14, words[1], words[2]))
    part = jnp.where(index < 7, index, jnp.where(index < 14, index - 7, index - 14))
    return (word >> (4 * part)) & 15


def plain(x):
    return with_layout_constraint(x, Layout(major_to_minor=tuple(range(x.ndim))))


def reach(x, hop, size):
    return plain(lax.ppermute(plain(x), "dp", [(r, target(r, hop, size)) for r in range(size)]))


def spread(x, place, me):
    size = len(place)
    quarter = size // CLASSES
    mine = lookup(place, me)
    take = lambda which: lax.dynamic_slice_in_dim(x, which * quarter, quarter, axis=1)
    landed = [
        reach(take(lookup([place[target(r, hop, size)] // quarter for r in range(size)], me)), hop, size) for hop in HOPS
    ]
    held = plain(lax.optimization_barrier(take(mine // quarter) + landed[0] + landed[1] + landed[2]))
    half, last = (mine // 2) & 1, mine & 1
    two = lambda a, at: lax.dynamic_slice_in_dim(a, at, 2, axis=1)
    one = lambda a, at: lax.dynamic_index_in_dim(a, at, axis=1, keepdims=False)
    landed = reach(two(held, 2 - 2 * half), STEPS[0], size)
    out = one(held, 2 * half + 1 - last) + one(landed, 1 - last)
    keep = one(held, 2 * half + last) + one(landed, last)
    return lax.optimization_barrier(keep + reach(out, STEPS[1], size))


def row_statistics(part, row_state, mine):
    mats, count, width = part.shape
    squares = part * part + epsilon_one
    old = lax.dynamic_slice(row_state, (0, mine * count), (mats, count))
    row_sum = jnp.sum(lax.all_gather(jnp.sum(squares, axis=2), "col"), axis=0)
    row_fresh = decay_rate * old + (1.0 - decay_rate) * (row_sum / KV)
    col_part = jnp.sum(squares, axis=1)
    weighted = jnp.sum(squares * (1.0 / row_fresh)[:, :, None], axis=1)
    total = jnp.broadcast_to(jnp.sum(row_fresh, axis=1, keepdims=True), (mats, width))
    return jnp.concatenate([row_fresh, col_part, weighted, total], axis=0)


def col_statistics(sums, col_state):
    mats, width = col_state.shape
    sums = jnp.sum(lax.all_gather(sums, "row"), axis=0)
    row_total = sums[2 * mats :, 0]
    col_new = decay_rate * col_state + (1.0 - decay_rate) * (sums[:mats] / D)
    shares = lax.all_gather(sums[mats : 2 * mats] / col_new, "col")
    ratio = jnp.sum(shares, axis=(0, 2))
    mean_square = ratio * (row_total / D) / (D * KV)
    divisor = jnp.maximum(1.0, jnp.sqrt(mean_square) / clip_limit)
    scale = step_size * jnp.sqrt(row_total / D) / divisor
    return col_new, scale


def finish_kernel(class_ref, scale_ref, left_ref, right_ref, weight_ref, *refs):
    parts, out_ref, held, sems = refs[:CLASSES], refs[CLASSES], refs[CLASSES + 1], refs[CLASSES + 2]
    mats, _, blocks, rows, _ = weight_ref.shape
    right = [right_ref[m : m + 1] * scale_ref[m] for m in range(mats)]
    copies = []
    for k in range(CLASSES):
        which = class_ref[k]
        columns = jnp.transpose(left_ref[k])
        for b in range(blocks):
            for m in range(mats):
                factor = columns[:, b * mats + m : b * mats + m + 1] * right[m]
                held[k, m, b] = weight_ref[m, which, b] - parts[k][b, m * rows : (m + 1) * rows] * factor
        copies.append(pltpu.make_async_copy(held.at[k], out_ref.at[:, which], sems.at[k]))
        copies[-1].start()
    for copy in copies:
        copy.wait()


def finish(parts, weight, left, right, scale, classes):
    whole = lambda space: pl.BlockSpec(memory_space=space)
    mats, _, blocks, rows, width = weight.shape
    return pl.pallas_call(
        finish_kernel,
        in_specs=[whole(pltpu.SMEM)] * 2 + [whole(pltpu.VMEM)] * (3 + CLASSES),
        out_specs=whole(pltpu.HBM),
        out_shape=jax.ShapeDtypeStruct(weight.shape, weight.dtype),
        scratch_shapes=[
            pltpu.VMEM((CLASSES, mats, blocks, rows, width), weight.dtype),
            pltpu.SemaphoreType.DMA((CLASSES,)),
        ],
        compiler_params=pltpu.CompilerParams(vmem_limit_bytes=20 << 20),
        cost_estimate=pl.CostEstimate(flops=2**21, bytes_accessed=6 * 2**20, transcendentals=0),
    )(classes, scale, left, right, weight, *parts)


def local(gradients, weight, row_state, col_state):
    mats, rows, width = weight.shape
    size, me = lax.axis_size("dp"), lax.axis_index("dp")
    blocks, count = size // CLASSES, rows // size
    place = owners(size)
    part = spread(gradients.reshape(mats, size, count, width), place, me)
    extra = row_statistics(part, row_state, lookup(place, me))
    sent = jnp.concatenate([part.reshape(mats * count, width), extra], axis=0)
    members = [[place.index(c * blocks + b) for b in range(blocks)] for c in range(CLASSES)]
    own = lax.all_gather(sent, "dp", axis_index_groups=members)
    parts = [own] + [reach(own, hop, size) for hop in BACK]
    smalls = jnp.stack([p[:, mats * count :] for p in parts])
    classes = [lookup([p // blocks for p in place], me)]
    for hop in BACK:
        source = {target(r, hop, size): r for r in range(size)}
        classes.append(lookup([place[source[r]] // blocks for r in range(size)], me))
    placed = jnp.stack(classes)[None, :] == jnp.arange(CLASSES)[:, None]
    smalls_placed = jnp.sum(jnp.where(placed[:, :, None, None, None], smalls[None], 0.0), axis=1)
    row_new = jnp.transpose(smalls_placed[:, :, :mats].reshape(size, mats, count), (1, 0, 2)).reshape(mats, rows)
    col_new, scale = col_statistics(jnp.sum(smalls_placed[:, :, mats:], axis=(0, 1)), col_state)
    left = lax.rsqrt(smalls[:, :, :mats]).reshape(CLASSES, blocks * mats, count)
    split = weight.reshape(mats, CLASSES, blocks, count, width)
    new_weight = finish(parts, split, left, lax.rsqrt(col_new), scale, jnp.stack(classes))
    return (new_weight.reshape(weight.shape), row_new, col_new)


def solution(mesh):
    in_specs = (P("dp", None, "row", "col"), P(None, "row", "col"), P(None, "row"), P(None, "col"))
    out_specs = (P(None, "row", "col"), P(None, "row"), P(None, "col"))
    return jax.shard_map(local, mesh=mesh, in_specs=in_specs, out_specs=out_specs, check_vma=False)
```

```python
import functools

import jax
import jax.numpy as jnp
from jax import lax
from jax.experimental import pallas as pl
from jax.experimental.layout import Layout, with_layout_constraint
from jax.experimental.pallas import tpu as pltpu
from jax.sharding import PartitionSpec as P

D = 8192
KV = 1024

epsilon_one = 1e-30
decay_rate = 0.8
clip_limit = 1.0
step_size = 0.25

CLASSES = 4
HOPS = (2, -1, 1)
STEPS = (3, -5)
BACK = tuple(hop if hop % 2 else -hop for hop in HOPS)


def target(r, hop, size):
    return (r + hop if r % 2 == 0 else r - hop) % size


def owners(size):
    place, free = {}, 0
    for r in range(0, size, 2):
        if r not in place:
            other = target(r, STEPS[0], size)
            for q in (target(r, STEPS[1], size), r, other, target(other, STEPS[1], size)):
                place[q], free = free, free + 1
    return [place[r] for r in range(size)]


def lookup(table, index):
    words = [sum(v << (4 * i) for i, v in enumerate(table[k : k + 7])) for k in (0, 7, 14)]
    word = jnp.where(index < 7, words[0], jnp.where(index < 14, words[1], words[2]))
    part = jnp.where(index < 7, index, jnp.where(index < 14, index - 7, index - 14))
    return (word >> (4 * part)) & 15


def plain(x):
    return with_layout_constraint(x, Layout(major_to_minor=tuple(range(x.ndim))))


def reach(x, hop, size):
    return plain(lax.ppermute(plain(x), "dp", [(r, target(r, hop, size)) for r in range(size)]))


def spread(x, place, me):
    size = len(place)
    quarter = size // CLASSES
    mine = lookup(place, me)
    take = lambda which: lax.dynamic_slice_in_dim(x, which * quarter, quarter, axis=1)
    landed = [
        reach(take(lookup([place[target(r, hop, size)] // quarter for r in range(size)], me)), hop, size) for hop in HOPS
    ]
    held = plain(lax.optimization_barrier(take(mine // quarter) + landed[0] + landed[1] + landed[2]))
    half, last = (mine // 2) & 1, mine & 1
    two = lambda a, at: lax.dynamic_slice_in_dim(a, at, 2, axis=1)
    one = lambda a, at: lax.dynamic_index_in_dim(a, at, axis=1, keepdims=False)
    landed = reach(two(held, 2 - 2 * half), STEPS[0], size)
    out = one(held, 2 * half + 1 - last) + one(landed, 1 - last)
    keep = one(held, 2 * half + last) + one(landed, last)
    return lax.optimization_barrier(keep + reach(out, STEPS[1], size))


def row_statistics(part, row_state, mine):
    mats, count, width = part.shape
    squares = part * part + epsilon_one
    old = lax.dynamic_slice(row_state, (0, mine * count), (mats, count))
    row_sum = jnp.sum(lax.all_gather(jnp.sum(squares, axis=2), "col"), axis=0)
    row_fresh = decay_rate * old + (1.0 - decay_rate) * (row_sum / KV)
    col_part = jnp.sum(squares, axis=1)
    weighted = jnp.sum(squares * (1.0 / row_fresh)[:, :, None], axis=1)
    total = jnp.broadcast_to(jnp.sum(row_fresh, axis=1, keepdims=True), (mats, width))
    return jnp.concatenate([row_fresh, col_part, weighted, total], axis=0)


def col_statistics(sums, col_state):
    mats, width = col_state.shape
    sums = jnp.sum(lax.all_gather(sums, "row"), axis=0)
    row_total = sums[2 * mats :, 0]
    col_new = decay_rate * col_state + (1.0 - decay_rate) * (sums[:mats] / D)
    shares = lax.all_gather(sums[mats : 2 * mats] / col_new, "col")
    ratio = jnp.sum(shares, axis=(0, 2))
    mean_square = ratio * (row_total / D) / (D * KV)
    divisor = jnp.maximum(1.0, jnp.sqrt(mean_square) / clip_limit)
    scale = step_size * jnp.sqrt(row_total / D) / divisor
    return col_new, scale


def finish_kernel(class_ref, scale_ref, left_ref, right_ref, weight_ref, *refs):
    parts, out_ref, held, sems = refs[:CLASSES], refs[CLASSES], refs[CLASSES + 1], refs[CLASSES + 2]
    mats, _, blocks, rows, _ = weight_ref.shape
    right = [right_ref[m : m + 1] * scale_ref[m] for m in range(mats)]
    copies = []
    for k in range(CLASSES):
        which = class_ref[k]
        columns = jnp.transpose(left_ref[k])
        for b in range(blocks):
            for m in range(mats):
                factor = columns[:, b * mats + m : b * mats + m + 1] * right[m]
                held[k, m, b] = weight_ref[m, which, b] - parts[k][b, m * rows : (m + 1) * rows] * factor
        copies.append(pltpu.make_async_copy(held.at[k], out_ref.at[:, which], sems.at[k]))
        copies[-1].start()
    for copy in copies:
        copy.wait()


def finish(parts, weight, left, right, scale, classes):
    whole = lambda space: pl.BlockSpec(memory_space=space)
    mats, _, blocks, rows, width = weight.shape
    return pl.pallas_call(
        finish_kernel,
        in_specs=[whole(pltpu.SMEM)] * 2 + [whole(pltpu.VMEM)] * (3 + CLASSES),
        out_specs=whole(pltpu.HBM),
        out_shape=jax.ShapeDtypeStruct(weight.shape, weight.dtype),
        scratch_shapes=[
            pltpu.VMEM((CLASSES, mats, blocks, rows, width), weight.dtype),
            pltpu.SemaphoreType.DMA((CLASSES,)),
        ],
        compiler_params=pltpu.CompilerParams(vmem_limit_bytes=20 << 20),
        cost_estimate=pl.CostEstimate(flops=2**21, bytes_accessed=6 * 2**20, transcendentals=0),
    )(classes, scale, left, right, weight, *parts)


def local(gradients, weight, row_state, col_state):
    mats, rows, width = weight.shape
    size, me = lax.axis_size("dp"), lax.axis_index("dp")
    blocks, count = size // CLASSES, rows // size
    place = owners(size)
    part = spread(gradients.reshape(mats, size, count, width), place, me)
    extra = row_statistics(part, row_state, lookup(place, me))
    sent = jnp.concatenate([part.reshape(mats * count, width), extra], axis=0)
    members = [[place.index(c * blocks + b) for b in range(blocks)] for c in range(CLASSES)]
    own = lax.all_gather(sent, "dp", axis_index_groups=members)
    small = lax.optimization_barrier(own[:, mats * count :])
    smalls = jnp.stack([small] + [reach(small, hop, size) for hop in BACK])
    parts = [own] + [reach(own, hop, size) for hop in BACK]
    classes = [lookup([p // blocks for p in place], me)]
    for hop in BACK:
        source = {target(r, hop, size): r for r in range(size)}
        classes.append(lookup([place[source[r]] // blocks for r in range(size)], me))
    placed = jnp.stack(classes)[None, :] == jnp.arange(CLASSES)[:, None]
    smalls_placed = jnp.sum(jnp.where(placed[:, :, None, None, None], smalls[None], 0.0), axis=1)
    row_new = jnp.transpose(smalls_placed[:, :, :mats].reshape(size, mats, count), (1, 0, 2)).reshape(mats, rows)
    col_new, scale = col_statistics(jnp.sum(smalls_placed[:, :, mats:], axis=(0, 1)), col_state)
    left = lax.rsqrt(smalls[:, :, :mats]).reshape(CLASSES, blocks * mats, count)
    split = weight.reshape(mats, CLASSES, blocks, count, width)
    new_weight = finish(parts, split, left, lax.rsqrt(col_new), scale, jnp.stack(classes))
    return (new_weight.reshape(weight.shape), row_new, col_new)


def solution(mesh):
    in_specs = (P("dp", None, "row", "col"), P(None, "row", "col"), P(None, "row"), P(None, "col"))
    out_specs = (P(None, "row", "col"), P(None, "row"), P(None, "col"))
    return jax.shard_map(local, mesh=mesh, in_specs=in_specs, out_specs=out_specs, check_vma=False)
```

```python
import functools

import jax
import jax.numpy as jnp
from jax import lax
from jax.experimental import pallas as pl
from jax.experimental.layout import Layout, with_layout_constraint
from jax.experimental.pallas import tpu as pltpu
from jax.sharding import PartitionSpec as P

D = 8192
KV = 1024

epsilon_one = 1e-30
decay_rate = 0.8
clip_limit = 1.0
step_size = 0.25

CLASSES = 4
HOPS = (2, 1, -1)
STEPS = (3, -5)
BACK = tuple(hop if hop % 2 else -hop for hop in HOPS)


def target(r, hop, size):
    return (r + hop if r % 2 == 0 else r - hop) % size


def owners(size):
    place, free = {}, 0
    for r in range(0, size, 2):
        if r not in place:
            other = target(r, STEPS[0], size)
            for q in (target(r, STEPS[1], size), r, other, target(other, STEPS[1], size)):
                place[q], free = free, free + 1
    return [place[r] for r in range(size)]


def lookup(table, index):
    words = [sum(v << (4 * i) for i, v in enumerate(table[k : k + 7])) for k in (0, 7, 14)]
    word = jnp.where(index < 7, words[0], jnp.where(index < 14, words[1], words[2]))
    part = jnp.where(index < 7, index, jnp.where(index < 14, index - 7, index - 14))
    return (word >> (4 * part)) & 15


def plain(x):
    return with_layout_constraint(x, Layout(major_to_minor=tuple(range(x.ndim))))


def reach(x, hop, size):
    return plain(lax.ppermute(plain(x), "dp", [(r, target(r, hop, size)) for r in range(size)]))


def spread(x, place, me):
    size = len(place)
    quarter = size // CLASSES
    mine = lookup(place, me)
    take = lambda which: lax.dynamic_slice_in_dim(x, which * quarter, quarter, axis=1)
    landed = [
        reach(take(lookup([place[target(r, hop, size)] // quarter for r in range(size)], me)), hop, size) for hop in HOPS
    ]
    held = plain(lax.optimization_barrier(take(mine // quarter) + landed[0] + landed[1] + landed[2]))
    half, last = (mine // 2) & 1, mine & 1
    two = lambda a, at: lax.dynamic_slice_in_dim(a, at, 2, axis=1)
    one = lambda a, at: lax.dynamic_index_in_dim(a, at, axis=1, keepdims=False)
    landed = reach(two(held, 2 - 2 * half), STEPS[0], size)
    out = one(held, 2 * half + 1 - last) + one(landed, 1 - last)
    keep = one(held, 2 * half + last) + one(landed, last)
    return lax.optimization_barrier(keep + reach(out, STEPS[1], size))


def row_statistics(part, row_state, mine):
    mats, count, width = part.shape
    squares = part * part + epsilon_one
    old = lax.dynamic_slice(row_state, (0, mine * count), (mats, count))
    row_sum = jnp.sum(lax.all_gather(jnp.sum(squares, axis=2), "col"), axis=0)
    row_fresh = decay_rate * old + (1.0 - decay_rate) * (row_sum / KV)
    col_part = jnp.sum(squares, axis=1)
    weighted = jnp.sum(squares * (1.0 / row_fresh)[:, :, None], axis=1)
    total = jnp.broadcast_to(jnp.sum(row_fresh, axis=1, keepdims=True), (mats, width))
    return jnp.concatenate([row_fresh, col_part, weighted, total], axis=0)


def col_statistics(sums, col_state):
    mats, width = col_state.shape
    sums = jnp.sum(lax.all_gather(sums, "row"), axis=0)
    row_total = sums[2 * mats :, 0]
    col_new = decay_rate * col_state + (1.0 - decay_rate) * (sums[:mats] / D)
    shares = lax.all_gather(sums[mats : 2 * mats] / col_new, "col")
    ratio = jnp.sum(shares, axis=(0, 2))
    mean_square = ratio * (row_total / D) / (D * KV)
    divisor = jnp.maximum(1.0, jnp.sqrt(mean_square) / clip_limit)
    scale = step_size * jnp.sqrt(row_total / D) / divisor
    return col_new, scale


def finish_kernel(class_ref, scale_ref, left_ref, right_ref, weight_ref, *refs):
    parts, out_ref, held, sems = refs[:CLASSES], refs[CLASSES], refs[CLASSES + 1], refs[CLASSES + 2]
    mats, _, blocks, rows, _ = weight_ref.shape
    right = [right_ref[m : m + 1] * scale_ref[m] for m in range(mats)]
    copies = []
    for k in range(CLASSES):
        which = class_ref[k]
        columns = jnp.transpose(left_ref[k])
        for b in range(blocks):
            for m in range(mats):
                factor = columns[:, b * mats + m : b * mats + m + 1] * right[m]
                held[k, m, b] = weight_ref[m, which, b] - parts[k][b, m * rows : (m + 1) * rows] * factor
        copies.append(pltpu.make_async_copy(held.at[k], out_ref.at[:, which], sems.at[k]))
        copies[-1].start()
    for copy in copies:
        copy.wait()


def finish(parts, weight, left, right, scale, classes):
    whole = lambda space: pl.BlockSpec(memory_space=space)
    mats, _, blocks, rows, width = weight.shape
    return pl.pallas_call(
        finish_kernel,
        in_specs=[whole(pltpu.SMEM)] * 2 + [whole(pltpu.VMEM)] * (3 + CLASSES),
        out_specs=whole(pltpu.HBM),
        out_shape=jax.ShapeDtypeStruct(weight.shape, weight.dtype),
        scratch_shapes=[
            pltpu.VMEM((CLASSES, mats, blocks, rows, width), weight.dtype),
            pltpu.SemaphoreType.DMA((CLASSES,)),
        ],
        compiler_params=pltpu.CompilerParams(vmem_limit_bytes=10 << 20),
        cost_estimate=pl.CostEstimate(flops=2**21, bytes_accessed=6 * 2**20, transcendentals=0),
    )(classes, scale, left, right, weight, *parts)


def local(gradients, weight, row_state, col_state):
    mats, rows, width = weight.shape
    size, me = lax.axis_size("dp"), lax.axis_index("dp")
    blocks, count = size // CLASSES, rows // size
    place = owners(size)
    part = spread(gradients.reshape(mats, size, count, width), place, me)
    extra = row_statistics(part, row_state, lookup(place, me))
    sent = jnp.concatenate([part.reshape(mats * count, width), extra], axis=0)
    members = [[place.index(c * blocks + b) for b in range(blocks)] for c in range(CLASSES)]
    own = lax.all_gather(sent, "dp", axis_index_groups=members)
    small = lax.optimization_barrier(own[:, mats * count :])
    smalls = jnp.stack([small] + [reach(small, hop, size) for hop in BACK])
    parts = [own] + [reach(own, hop, size) for hop in BACK]
    classes = [lookup([p // blocks for p in place], me)]
    for hop in BACK:
        source = {target(r, hop, size): r for r in range(size)}
        classes.append(lookup([place[source[r]] // blocks for r in range(size)], me))
    placed = jnp.stack(classes)[None, :] == jnp.arange(CLASSES)[:, None]
    smalls_placed = jnp.sum(jnp.where(placed[:, :, None, None, None], smalls[None], 0.0), axis=1)
    row_new = jnp.transpose(smalls_placed[:, :, :mats].reshape(size, mats, count), (1, 0, 2)).reshape(mats, rows)
    col_new, scale = col_statistics(jnp.sum(smalls_placed[:, :, mats:], axis=(0, 1)), col_state)
    left = lax.rsqrt(smalls[:, :, :mats]).reshape(CLASSES, blocks * mats, count)
    split = weight.reshape(mats, CLASSES, blocks, count, width)
    new_weight = finish(parts, split, left, lax.rsqrt(col_new), scale, jnp.stack(classes))
    return (new_weight.reshape(weight.shape), row_new, col_new)


def solution(mesh):
    in_specs = (P("dp", None, "row", "col"), P(None, "row", "col"), P(None, "row"), P(None, "col"))
    out_specs = (P(None, "row", "col"), P(None, "row"), P(None, "col"))
    return jax.shard_map(local, mesh=mesh, in_specs=in_specs, out_specs=out_specs, check_vma=False)
```
